768 devices in a mesh: fsdp: 16 (over y, x_hi), tp: 48 (over z, x_lo, core).
Axes of the slice: x: 4 (x_hi: 2, x_lo: 2; x = x_hi * 2 + x_lo), y: 8, z: 12, core: 2. Of those that a mesh axis runs over, the one named last changes fastest.
Arguments:
- tokens: bfloat16 [4608, 8192], P('fsdp'), may hold values from -6 to 6
- norm_gain: bfloat16 [8192], replicated, may hold values from 0.099609375 to 1.8984375
- base: bfloat16 [8192, 18432], P(None, 'tp')
- trained: bfloat16 [8192, 18432], P('fsdp', 'tp')
- exponents: int32 [64, 144], replicated, may hold values from -19 to -14
Outputs:
- gated: bfloat16 [4608, 18432], P('fsdp', 'tp')
The draws below stay inside these ranges and needn't reach their ends.
All inputs are finite; a program needn't handle non-finite values.
Results may differ from the reference program's by a relative error of at most 0.0053.
Values may be sent and summed in bfloat16 or wider, within the bound.
No kernel may reach another device: no remote copies, remote signals or barrier semaphores. Data moves between devices by JAX's collectives and lax.ppermute only.
A program may use at most 64 MiB of HBM per device.

```python
import jax
import jax.numpy as jnp
from jax import lax

D = 8192
FFW = 18432
BLK = 128
TOKENS = 4608


def shared_blocks(key):
    blocks_d = D // BLK
    blocks_f = FFW // BLK
    base_key = jax.random.fold_in(key, 11)
    level_key = jax.random.fold_in(key, 12)
    lower_key = jax.random.fold_in(key, 13)
    base_wide = jax.random.normal(base_key, (D, FFW), jnp.float32) * D ** (-0.5)
    base_wide = jnp.clip(base_wide, -6.0 * D ** (-0.5), 6.0 * D ** (-0.5))
    base_short = base_wide.astype(jnp.bfloat16)
    true_level = jax.random.randint(level_key, (blocks_d, blocks_f), -18, -13)
    lowered = (jax.random.randint(lower_key, (blocks_d, blocks_f), 0, 8) == 0).astype(jnp.int32)
    row_index = jnp.arange(blocks_d, dtype=jnp.int32)[:, None]
    col_index = jnp.arange(blocks_f, dtype=jnp.int32)[None, :]
    first_block = (row_index == 0) & (col_index == 0)
    second_block = (row_index == 0) & (col_index == 1)
    true_level = jnp.where(first_block, -18, jnp.where(second_block, -14, true_level))
    lowered = jnp.where(first_block, 1, jnp.where(second_block, 0, lowered))
    given_level = (true_level - lowered).astype(jnp.int32)
    return (base_short, true_level.astype(jnp.int32), given_level)


def draw_base(key, part):
    base_short, true_level, given_level = shared_blocks(key)
    return base_short


def draw_exponents(key, part):
    base_short, true_level, given_level = shared_blocks(key)
    return given_level


def draw_trained(key, part):
    base_short, true_level, given_level = shared_blocks(key)
    key = jax.random.fold_in(key, 21)
    blocks_d = D // BLK
    blocks_f = FFW // BLK
    value_key = jax.random.fold_in(key, 1)
    row_key = jax.random.fold_in(key, 2)
    col_key = jax.random.fold_in(key, 3)
    peak_key = jax.random.fold_in(key, 4)
    sign_key = jax.random.fold_in(key, 5)
    units = jnp.clip(jax.random.normal(value_key, (blocks_d, BLK, blocks_f, BLK), jnp.float32) * 150.0, -400.0, 400.0)
    peak_row = jax.random.randint(row_key, (blocks_d, blocks_f), 0, BLK)
    peak_col = jax.random.randint(col_key, (blocks_d, blocks_f), 0, BLK)
    peak_size = jax.random.uniform(peak_key, (blocks_d, blocks_f), jnp.float32, 300.0, 440.0)
    peak_sign = jnp.where(jax.random.randint(sign_key, (blocks_d, blocks_f), 0, 2) == 0, -1.0, 1.0).astype(jnp.float32)
    inner = jnp.arange(BLK, dtype=jnp.int32)
    at_peak = (inner[None, :, None, None] == peak_row[:, None, :, None]) & (inner[None, None, None, :] == peak_col[:, None, :, None])
    units = jnp.where(at_peak, (peak_size * peak_sign)[:, None, :, None], units)
    scale = jnp.exp2(true_level.astype(jnp.float32))[:, None, :, None]
    delta = (units * scale).reshape(D, FFW)
    return (base_short.astype(jnp.float32) + delta).astype(jnp.bfloat16)


def block_scale(own_key, extent, pieces, least, high):
    def one(position, blocks):
        steps = jax.random.uniform(jax.random.fold_in(jax.random.fold_in(own_key, 6), position), (blocks,), jnp.float32, least / len(pieces), high / len(pieces))
        return jnp.repeat(jnp.exp(steps), extent[position] // blocks).reshape((-1,) + (1,) * (len(extent) - position - 1))

    factor_of = one(*pieces[0])
    for cut in pieces[1:]:
        factor_of = factor_of * one(*cut)
    return factor_of


def normal_values(own_key, extent, scale, limit, shards=(), kind=jnp.bfloat16):
    result = jax.random.normal(own_key, extent, jnp.float32) * scale
    if len(shards) > 0:
        result = block_scale(own_key, extent, shards, -0.22, 0.18) * result
    return jnp.clip(result, min=-limit, max=limit).astype(kind)


def setup_inputs(seed: int = 0) -> dict:
    splits = jax.random.split(jax.random.key(seed), 6)
    tokens = normal_values(splits[0], (TOKENS, D), 1.0, 6.0, ((0, 16),))
    norm_gain = jnp.clip(1.0 + 0.18 * jax.random.normal(splits[1], (D,), jnp.float32), 0.099609375, 1.8984375).astype(jnp.bfloat16)
    base = draw_base(jax.random.fold_in(splits[5], 71), 0)
    trained = draw_trained(jax.random.fold_in(splits[5], 71), 0)
    exponents = draw_exponents(jax.random.fold_in(splits[5], 71), 0)
    return {"tokens": tokens, "norm_gain": norm_gain, "base": base, "trained": trained, "exponents": exponents}


clip_limit = 448.0
norm_epsilon = 1e-06
exponent_floor = -19

def power_table(exponents):
    scale = jnp.zeros(exponents.shape, jnp.float32)
    for offset in range(6):
        level = exponent_floor + offset
        scale = scale + jnp.where(exponents == level, jnp.float32(2.0 ** level), jnp.float32(0.0)).astype(jnp.float32)
    return scale

def reference(tokens, norm_gain, base, trained, exponents):
    rows_wide = tokens.astype(jnp.float32)
    mean_square = lax.optimization_barrier(jnp.mean(rows_wide * rows_wide, axis=1, keepdims=True))
    normed = (rows_wide * lax.rsqrt(mean_square + norm_epsilon) * norm_gain.astype(jnp.float32)).astype(jnp.bfloat16)
    table = power_table(exponents)
    blocks_d = D // BLK
    blocks_f = FFW // BLK
    scale = table[:, None, :, None]
    base_wide = base.astype(jnp.float32).reshape(blocks_d, BLK, blocks_f, BLK)
    delta = trained.astype(jnp.float32).reshape(blocks_d, BLK, blocks_f, BLK) - base_wide
    coded = jnp.clip(delta / scale, -clip_limit, clip_limit).astype(jnp.bfloat16)
    coded = lax.optimization_barrier(coded)
    weight = (base_wide + coded.astype(jnp.float32) * scale).astype(jnp.bfloat16).reshape(D, FFW)
    product = jnp.dot(normed, weight, preferred_element_type=jnp.float32)
    return jax.nn.silu(product).astype(jnp.bfloat16)
```

```python
import jax
import jax.numpy as jnp
from jax import lax
from jax.experimental import pallas as pl
from jax.experimental.pallas import tpu as pltpu
from jax.sharding import PartitionSpec as P

BLK = 128

clip_limit = 448.0
norm_epsilon = 1e-06
exponent_floor = -19
lift = 2.0**21


def power(exponent):
    scale = jnp.float32(2.0**exponent_floor)
    for level in range(exponent_floor + 1, exponent_floor + 6):
        scale = jnp.where(exponent == level, jnp.float32(2.0**level), scale)
    return scale


def prepare_kernel(tokens, gain, base, trained, exponents, update, part, x, y, g, b, t, e, sems):
    own_rows, columns = trained.shape
    half_rows, half = part.shape
    pairs = half // own_rows
    f = lax.axis_index("fsdp")
    tp = lax.axis_index("tp")
    side = lax.rem(f, 2)
    core = lax.rem(tp, 2)
    row_blocks, col_blocks = own_rows // BLK, columns // BLK
    first_row = pl.multiple_of(core * half_rows, 16)
    exp_row = pl.multiple_of((f * row_blocks) // 8 * 8, 8)
    exp_copy = pltpu.make_async_copy(exponents.at[pl.ds(exp_row, 8)], e, sems.at[0])
    exp_copy.start()
    base_copy = pltpu.make_async_copy(base.at[pl.ds(pl.multiple_of(f * own_rows, own_rows), own_rows)], b, sems.at[1])
    base_copy.start()
    trained_copy = pltpu.make_async_copy(trained, t, sems.at[2])
    trained_copy.start()
    gain_copy = pltpu.make_async_copy(gain, g, sems.at[3])
    gain_copy.start()

    def column(p):
        return pl.multiple_of((2 * p + 1 - side) * own_rows, own_rows)

    ins = [
        pltpu.make_async_copy(
            tokens.at[pl.ds(first_row, half_rows), pl.ds(column(p), own_rows)],
            x.at[:, pl.ds(p * own_rows, own_rows)],
            sems.at[4 + p],
        )
        for p in range(pairs)
    ]
    for copy in ins:
        copy.start()
    exp_copy.wait()
    base_copy.wait()
    trained_copy.wait()
    for i in range(row_blocks):
        for j in range(col_blocks):
            exponent = e[lax.rem(f * row_blocks, 8) + i, tp * col_blocks + j]
            scale = power(exponent)
            spot = (pl.ds(i * BLK, BLK), pl.ds(j * BLK, BLK))
            diff = t[spot].astype(jnp.float32) - b[spot].astype(jnp.float32)
            coded = jnp.clip(diff * (1.0 / scale), -clip_limit, clip_limit).astype(jnp.bfloat16)
            update[spot] = (coded.astype(jnp.float32) * (scale * lift)).astype(jnp.bfloat16)
    gain_copy.wait()
    outs = [
        pltpu.make_async_copy(
            y.at[:, pl.ds(p * own_rows, own_rows)], part.at[:, pl.ds(p * own_rows, own_rows)], sems.at[4 + pairs + p]
        )
        for p in range(pairs)
    ]
    for p in range(pairs):
        ins[p].wait()
        spot = (slice(None), pl.ds(p * own_rows, own_rows))
        row = g[:, pl.ds(column(p), own_rows)].astype(jnp.float32)
        y[spot] = (x[spot].astype(jnp.float32) * row).astype(jnp.bfloat16)
        outs[p].start()
    for copy in outs:
        copy.wait()


def prepare(tokens, gain, base, trained, exponents):
    rows, depth = tokens.shape
    half_rows, half = rows // 2, depth // 2
    own_rows, columns = trained.shape
    pairs = half // own_rows
    hbm = pl.BlockSpec(memory_space=pltpu.HBM)
    return pl.pallas_call(
        prepare_kernel,
        out_shape=(
            jax.ShapeDtypeStruct((own_rows, columns), jnp.bfloat16),
            jax.ShapeDtypeStruct((half_rows, half), jnp.bfloat16),
        ),
        in_specs=[hbm] * 5,
        out_specs=(pl.BlockSpec(memory_space=pltpu.VMEM), hbm),
        scratch_shapes=[
            pltpu.VMEM((half_rows, half), jnp.bfloat16),
            pltpu.VMEM((half_rows, half), jnp.bfloat16),
            pltpu.VMEM((1, depth), jnp.bfloat16),
            pltpu.VMEM((own_rows, columns), jnp.bfloat16),
            pltpu.VMEM((own_rows, columns), jnp.bfloat16),
            pltpu.SMEM((8, exponents.shape[1]), jnp.int32),
            pltpu.SemaphoreType.DMA((4 + 2 * pairs,)),
        ],
        compiler_params=pltpu.CompilerParams(vmem_limit_bytes=16 * 2**20),
        cost_estimate=pl.CostEstimate(flops=4 * 10**6, bytes_accessed=6 * 10**6, transcendentals=0),
    )(tokens, gain, base, trained, exponents)


def far_kernel(base, delta, got, rest, partial, total):
    step = pl.program_id(0)
    core = lax.rem(lax.axis_index("tp"), 2)
    half_rows = got.shape[0]

    @pl.when(step == 0)
    def _():
        total[...] = jnp.zeros_like(total)

    count, _, own_rows, columns = base.shape
    for i in range(count):
        spot = pl.ds(i * own_rows, own_rows)
        weight = (base[i, 0].astype(jnp.float32) + delta[spot].astype(jnp.float32)).astype(jnp.bfloat16)
        total[0] += jnp.dot(got[:, spot], weight, preferred_element_type=jnp.float32)
        total[1] += jnp.dot(rest[:, spot], weight, preferred_element_type=jnp.float32)

    @pl.when(step == pl.num_programs(0) - 1)
    def _():
        partial[pl.ds(pl.multiple_of(core * half_rows, 16), half_rows)] = total[0].astype(jnp.bfloat16)
        partial[pl.ds(pl.multiple_of((1 - core) * half_rows, 16), half_rows)] = total[1].astype(jnp.bfloat16)


def far_product(base4, delta, got, rest):
    pairs, _, own_rows, columns = base4.shape
    half_rows = got.shape[0]
    count = 2
    return pl.pallas_call(
        far_kernel,
        grid=(pairs // count,),
        out_shape=jax.ShapeDtypeStruct((2 * half_rows, columns), jnp.bfloat16),
        in_specs=[
            pl.BlockSpec((count, 1, own_rows, columns), lambda s: (s, lax.rem(lax.axis_index("fsdp"), 2), 0, 0)),
            pl.BlockSpec((count * own_rows, columns), lambda s: (s, 0)),
            pl.BlockSpec((half_rows, count * own_rows), lambda s: (0, s)),
            pl.BlockSpec((half_rows, count * own_rows), lambda s: (0, s)),
        ],
        out_specs=pl.BlockSpec((2 * half_rows, columns), lambda s: (0, 0)),
        scratch_shapes=[pltpu.VMEM((2, half_rows, columns), jnp.float32)],
        compiler_params=pltpu.CompilerParams(vmem_limit_bytes=16 * 2**20),
        cost_estimate=pl.CostEstimate(flops=10**9, bytes_accessed=9 * 10**6, transcendentals=0),
    )(base4, delta, got, rest)


def near_kernel(tokens, gain, base, delta, product, factor, x, b, d, sems):
    pairs, own_rows, columns = b.shape
    rows, depth = x.shape
    side = lax.rem(lax.axis_index("fsdp"), 2)
    width = 2 * own_rows
    token_copies = [
        pltpu.make_async_copy(
            tokens.at[:, pl.ds(p * width, width)], x.at[:, pl.ds(p * width, width)], sems.at[p]
        )
        for p in range(pairs)
    ]
    base_copies = [pltpu.make_async_copy(base.at[p, side], b.at[p], sems.at[pairs + p]) for p in range(pairs)]
    delta_copies = [
        pltpu.make_async_copy(delta.at[pl.ds(p * own_rows, own_rows)], d.at[p], sems.at[2 * pairs + p])
        for p in range(pairs)
    ]
    for copy in token_copies:
        copy.start()
    for p in range(pairs):
        base_copies[p].start()
        delta_copies[p].start()
    squares = jnp.zeros((rows, BLK), jnp.float32)
    for p in range(pairs):
        token_copies[p].wait()
        for c in range(width // BLK):
            wide = x[:, pl.ds(p * width + c * BLK, BLK)].astype(jnp.float32)
            squares += wide * wide
    mean_square = jnp.sum(squares, axis=1, keepdims=True) * (1.0 / depth)
    scale = lax.rsqrt(mean_square + norm_epsilon)
    factor[...] = jnp.broadcast_to(scale, factor.shape)
    total = jnp.zeros((rows, columns), jnp.float32)
    for p in range(pairs):
        base_copies[p].wait()
        delta_copies[p].wait()
        weight = (b[p].astype(jnp.float32) + d[p].astype(jnp.float32)).astype(jnp.bfloat16)
        spot = pl.ds(pl.multiple_of((2 * p + side) * own_rows, own_rows), own_rows)
        row = gain[:, spot].astype(jnp.float32)
        normed = (x[:, spot].astype(jnp.float32) * scale * row).astype(jnp.bfloat16)
        total += jnp.dot(normed, weight, preferred_element_type=jnp.float32)
    product[...] = total


def near_product(tokens, gain, base4, delta):
    pairs, _, own_rows, columns = base4.shape
    rows, depth = tokens.shape
    hbm = pl.BlockSpec(memory_space=pl.ANY)
    vmem = pl.BlockSpec(memory_space=pltpu.VMEM)
    return pl.pallas_call(
        near_kernel,
        out_shape=(
            jax.ShapeDtypeStruct((rows, columns), jnp.float32),
            jax.ShapeDtypeStruct((rows, BLK), jnp.float32),
        ),
        in_specs=[hbm, vmem, hbm, hbm],
        out_specs=(vmem, vmem),
        scratch_shapes=[
            pltpu.VMEM((rows, depth), jnp.bfloat16),
            pltpu.VMEM((pairs, own_rows, columns), jnp.bfloat16),
            pltpu.VMEM((pairs, own_rows, columns), jnp.bfloat16),
            pltpu.SemaphoreType.DMA((3 * pairs,)),
        ],
        compiler_params=pltpu.CompilerParams(vmem_limit_bytes=24 * 2**20),
        cost_estimate=pl.CostEstimate(flops=10**9, bytes_accessed=12 * 10**6, transcendentals=0),
    )(tokens, gain, base4, delta)


def body(tokens, norm_gain, base, trained, exponents):
    rows, depth = tokens.shape
    columns = base.shape[1]
    own_rows = trained.shape[0]
    sides = depth // own_rows
    pairs = sides // 2
    gain = norm_gain.reshape(1, depth)
    across = [(i, i ^ 1) for i in range(sides)]
    cores = [(i, i ^ 1) for i in range(lax.axis_size("tp"))]
    groups = [list(range(0, sides, 2)), list(range(1, sides, 2))]
    update, part = prepare(tokens, gain, base, trained, exponents)
    got = lax.ppermute(part, "fsdp", across)
    wide = lax.all_gather(update.astype(jnp.float16), "fsdp", axis=0, tiled=True, axis_index_groups=groups)
    wide, got = lax.optimization_barrier((wide, got))
    rest = lax.ppermute(got, "tp", cores)
    delta = (wide.astype(jnp.float32) * (1.0 / lift)).astype(jnp.bfloat16)
    base4 = base.reshape(pairs, 2, own_rows, columns)
    far = lax.ppermute(far_product(base4, delta, got, rest), "fsdp", across)
    near, factor = near_product(tokens, gain, base4, delta)
    product = near + far.astype(jnp.float32) * factor[:, :1]
    return jax.nn.silu(product).astype(jnp.bfloat16)


def solution(mesh):
    placed = (P("fsdp", None), P(), P(None, "tp"), P("fsdp", "tp"), P())
    return jax.shard_map(
        body, mesh=mesh, in_specs=placed, out_specs=P("fsdp", "tp"), check_vma=False
    )
```

```python
import jax
import jax.numpy as jnp
from jax import lax
from jax.experimental import pallas as pl
from jax.experimental.pallas import tpu as pltpu
from jax.sharding import PartitionSpec as P

BLK = 128

clip_limit = 448.0
norm_epsilon = 1e-06
exponent_floor = -19
lift = 2.0**21


def power(exponent):
    scale = jnp.float32(2.0**exponent_floor)
    for level in range(exponent_floor + 1, exponent_floor + 6):
        scale = jnp.where(exponent == level, jnp.float32(2.0**level), scale)
    return scale


def prepare_kernel(tokens, base, trained, exponents, update, part, b, t, e, sems):
    own_rows, columns = trained.shape
    half_rows, half = part.shape
    pairs = half // own_rows
    f = lax.axis_index("fsdp")
    tp = lax.axis_index("tp")
    side = lax.rem(f, 2)
    core = lax.rem(tp, 2)
    row_blocks, col_blocks = own_rows // BLK, columns // BLK
    first_row = pl.multiple_of(core * half_rows, 16)
    exp_row = pl.multiple_of((f * row_blocks) // 8 * 8, 8)
    exp_copy = pltpu.make_async_copy(exponents.at[pl.ds(exp_row, 8)], e, sems.at[0])
    exp_copy.start()
    base_copy = pltpu.make_async_copy(base.at[pl.ds(pl.multiple_of(f * own_rows, own_rows), own_rows)], b, sems.at[1])
    base_copy.start()
    trained_copy = pltpu.make_async_copy(trained, t, sems.at[2])
    trained_copy.start()
    token_copies = []
    for p in range(pairs):
        column = pl.multiple_of((2 * p + 1 - side) * own_rows, own_rows)
        copy = pltpu.make_async_copy(
            tokens.at[pl.ds(first_row, half_rows), pl.ds(column, own_rows)],
            part.at[:, pl.ds(p * own_rows, own_rows)],
            sems.at[3 + p],
        )
        copy.start()
        token_copies.append(copy)
    exp_copy.wait()
    base_copy.wait()
    trained_copy.wait()
    for i in range(row_blocks):
        for j in range(col_blocks):
            exponent = e[lax.rem(f * row_blocks, 8) + i, tp * col_blocks + j]
            scale = power(exponent)
            spot = (pl.ds(i * BLK, BLK), pl.ds(j * BLK, BLK))
            diff = t[spot].astype(jnp.float32) - b[spot].astype(jnp.float32)
            coded = jnp.clip(diff * (1.0 / scale), -clip_limit, clip_limit).astype(jnp.bfloat16)
            update[spot] = (coded.astype(jnp.float32) * (scale * lift)).astype(jnp.bfloat16)
    for copy in token_copies:
        copy.wait()


def prepare(tokens, base, trained, exponents):
    rows, depth = tokens.shape
    half_rows, half = rows // 2, depth // 2
    own_rows, columns = trained.shape
    pairs = half // own_rows
    hbm = pl.BlockSpec(memory_space=pl.ANY)
    return pl.pallas_call(
        prepare_kernel,
        out_shape=(
            jax.ShapeDtypeStruct((own_rows, columns), jnp.bfloat16),
            jax.ShapeDtypeStruct((half_rows, half), jnp.bfloat16),
        ),
        in_specs=[hbm] * 4,
        out_specs=(pl.BlockSpec(memory_space=pltpu.VMEM), hbm),
        scratch_shapes=[
            pltpu.VMEM((own_rows, columns), jnp.bfloat16),
            pltpu.VMEM((own_rows, columns), jnp.bfloat16),
            pltpu.SMEM((8, exponents.shape[1]), jnp.int32),
            pltpu.SemaphoreType.DMA((3 + pairs,)),
        ],
        compiler_params=pltpu.CompilerParams(vmem_limit_bytes=60 * 2**20),
        cost_estimate=pl.CostEstimate(flops=4 * 10**6, bytes_accessed=6 * 10**6, transcendentals=0),
    )(tokens, base, trained, exponents)


def far_kernel(base, delta, got, rest, gain, partial, total):
    step = pl.program_id(0)
    core = lax.rem(lax.axis_index("tp"), 2)
    half_rows = got.shape[0]

    @pl.when(step == 0)
    def _():
        total[...] = jnp.zeros_like(total)

    count, _, own_rows, columns = base.shape
    for i in range(count):
        spot = pl.ds(i * own_rows, own_rows)
        row = gain[i, 0].astype(jnp.float32)
        weight = (base[i, 0].astype(jnp.float32) + delta[spot].astype(jnp.float32)).astype(jnp.bfloat16)
        for k, x in enumerate((got, rest)):
            raised = (x[:, spot].astype(jnp.float32) * row).astype(jnp.bfloat16)
            total[k] += jnp.dot(raised, weight, preferred_element_type=jnp.float32)

    @pl.when(step == pl.num_programs(0) - 1)
    def _():
        partial[pl.ds(pl.multiple_of(core * half_rows, 16), half_rows)] = total[0].astype(jnp.bfloat16)
        partial[pl.ds(pl.multiple_of((1 - core) * half_rows, 16), half_rows)] = total[1].astype(jnp.bfloat16)


def far_product(base4, delta, got, rest, gain4):
    pairs, _, own_rows, columns = base4.shape
    half_rows = got.shape[0]
    count = 2
    return pl.pallas_call(
        far_kernel,
        grid=(pairs // count,),
        out_shape=jax.ShapeDtypeStruct((2 * half_rows, columns), jnp.bfloat16),
        in_specs=[
            pl.BlockSpec((count, 1, own_rows, columns), lambda s: (s, lax.rem(lax.axis_index("fsdp"), 2), 0, 0)),
            pl.BlockSpec((count * own_rows, columns), lambda s: (s, 0)),
            pl.BlockSpec((half_rows, count * own_rows), lambda s: (0, s)),
            pl.BlockSpec((half_rows, count * own_rows), lambda s: (0, s)),
            pl.BlockSpec((count, 1, 1, own_rows), lambda s: (s, lax.rem(lax.axis_index("fsdp"), 2), 0, 0)),
        ],
        out_specs=pl.BlockSpec((2 * half_rows, columns), lambda s: (0, 0)),
        scratch_shapes=[pltpu.VMEM((2, half_rows, columns), jnp.float32)],
        compiler_params=pltpu.CompilerParams(vmem_limit_bytes=16 * 2**20),
        cost_estimate=pl.CostEstimate(flops=10**9, bytes_accessed=9 * 10**6, transcendentals=0),
    )(base4, delta, got, rest, gain4)


def factor_kernel(tokens, after, factor, squares):
    step = pl.program_id(0)

    @pl.when(step == 0)
    def _():
        squares[...] = jnp.zeros_like(squares)

    rows, width = tokens.shape
    found = squares[...]
    for c in range(width // BLK):
        wide = tokens[:, pl.ds(c * BLK, BLK)].astype(jnp.float32)
        found += wide * wide
    squares[...] = found

    @pl.when(step == pl.num_programs(0) - 1)
    def _():
        mean_square = jnp.sum(found, axis=1, keepdims=True) * (1.0 / (width * pl.num_programs(0)))
        factor[...] = jnp.broadcast_to(lax.rsqrt(mean_square + norm_epsilon), factor.shape)


def row_factor(tokens, after):
    rows, depth = tokens.shape
    steps = 4
    return pl.pallas_call(
        factor_kernel,
        grid=(steps,),
        out_shape=jax.ShapeDtypeStruct((rows, BLK), jnp.float32),
        in_specs=[pl.BlockSpec((rows, depth // steps), lambda s: (0, s)), pl.BlockSpec(memory_space=pl.ANY)],
        out_specs=pl.BlockSpec((rows, BLK), lambda s: (0, 0)),
        scratch_shapes=[pltpu.VMEM((rows, BLK), jnp.float32)],
        compiler_params=pltpu.CompilerParams(vmem_limit_bytes=16 * 2**20),
        cost_estimate=pl.CostEstimate(flops=5 * 10**6, bytes_accessed=5 * 10**6, transcendentals=0),
    )(tokens, after)


def near_kernel(base, delta, gain, factor, *refs):
    *tokens, product = refs
    step = pl.program_id(0)

    @pl.when(step == 0)
    def _():
        product[...] = jnp.zeros_like(product)

    count, _, own_rows, columns = base.shape
    scale = factor[:, :1]
    for i in range(count):
        spot = pl.ds(i * own_rows, own_rows)
        row = gain[i, 0].astype(jnp.float32)
        weight = (base[i, 0].astype(jnp.float32) + delta[spot].astype(jnp.float32)).astype(jnp.bfloat16)
        normed = (tokens[i][...].astype(jnp.float32) * scale * row).astype(jnp.bfloat16)
        product[...] += jnp.dot(normed, weight, preferred_element_type=jnp.float32)


def near_product(tokens, gain4, base4, delta, factor):
    pairs, _, own_rows, columns = base4.shape
    rows, depth = tokens.shape
    count = 2

    def side():
        return lax.rem(lax.axis_index("fsdp"), 2)

    return pl.pallas_call(
        near_kernel,
        grid=(pairs // count,),
        out_shape=jax.ShapeDtypeStruct((rows, columns), jnp.float32),
        in_specs=[
            pl.BlockSpec((count, 1, own_rows, columns), lambda s: (s, side(), 0, 0)),
            pl.BlockSpec((count * own_rows, columns), lambda s: (s, 0)),
            pl.BlockSpec((count, 1, 1, own_rows), lambda s: (s, side(), 0, 0)),
            pl.BlockSpec((rows, BLK), lambda s: (0, 0)),
        ]
        + [pl.BlockSpec((rows, own_rows), lambda s, i=i: (0, 2 * (count * s + i) + side())) for i in range(count)],
        out_specs=pl.BlockSpec((rows, columns), lambda s: (0, 0)),
        compiler_params=pltpu.CompilerParams(vmem_limit_bytes=16 * 2**20),
        cost_estimate=pl.CostEstimate(flops=10**9, bytes_accessed=9 * 10**6, transcendentals=0),
    )(base4, delta, gain4, factor, *[tokens] * count)


def body(tokens, norm_gain, base, trained, exponents):
    rows, depth = tokens.shape
    columns = base.shape[1]
    own_rows = trained.shape[0]
    sides = depth // own_rows
    pairs = sides // 2
    across = [(i, i ^ 1) for i in range(sides)]
    cores = [(i, i ^ 1) for i in range(lax.axis_size("tp"))]
    groups = [list(range(0, sides, 2)), list(range(1, sides, 2))]
    update, part = prepare(tokens, base, trained, exponents)
    got = lax.ppermute(part, "fsdp", across)
    wide = lax.all_gather(update.astype(jnp.float16), "fsdp", axis=0, tiled=True, axis_index_groups=groups)
    wide, got, late_gain = lax.optimization_barrier((wide, got, norm_gain))
    gain4 = late_gain.reshape(pairs, 2, 1, own_rows)
    rest = lax.ppermute(got, "tp", cores)
    delta = (wide.astype(jnp.float32) * (1.0 / lift)).astype(jnp.bfloat16)
    base4 = base.reshape(pairs, 2, own_rows, columns)
    partial = far_product(base4, delta, got, rest, gain4)
    far = lax.ppermute(partial, "fsdp", across)
    factor = row_factor(tokens, partial)
    near = near_product(tokens, gain4, base4, delta, factor)
    product = near + far.astype(jnp.float32) * factor[:, :1]
    return jax.nn.silu(product).astype(jnp.bfloat16)


def solution(mesh):
    placed = (P("fsdp", None), P(), P(None, "tp"), P("fsdp", "tp"), P())
    return jax.shard_map(
        body, mesh=mesh, in_specs=placed, out_specs=P("fsdp", "tp"), check_vma=False
    )
```

```python
import jax
import jax.numpy as jnp
from jax import lax
from jax.experimental import pallas as pl
from jax.experimental.pallas import tpu as pltpu
from jax.sharding import PartitionSpec as P

BLK = 128

clip_limit = 448.0
norm_epsilon = 1e-06
exponent_floor = -19
lift = 2.0**21


def power(exponent):
    scale = jnp.float32(2.0**exponent_floor)
    for level in range(exponent_floor + 1, exponent_floor + 6):
        scale = jnp.where(exponent == level, jnp.float32(2.0**level), scale)
    return scale


def prepare_kernel(tokens, base, trained, exponents, update, part, x, b, t, e, sems):
    own_rows, columns = trained.shape
    half_rows, half = part.shape
    pairs = half // own_rows
    f = lax.axis_index("fsdp")
    tp = lax.axis_index("tp")
    side = lax.rem(f, 2)
    core = lax.rem(tp, 2)
    row_blocks, col_blocks = own_rows // BLK, columns // BLK
    first_row = pl.multiple_of(core * half_rows, 16)
    exp_row = pl.multiple_of((f * row_blocks) // 8 * 8, 8)
    exp_copy = pltpu.make_async_copy(exponents.at[pl.ds(exp_row, 8)], e, sems.at[0])
    exp_copy.start()
    base_copy = pltpu.make_async_copy(base.at[pl.ds(pl.multiple_of(f * own_rows, own_rows), own_rows)], b, sems.at[1])
    base_copy.start()
    trained_copy = pltpu.make_async_copy(trained, t, sems.at[2])
    trained_copy.start()
    token_copies = []
    for p in range(pairs):
        column = pl.multiple_of((2 * p + 1 - side) * own_rows, own_rows)
        copy = pltpu.make_async_copy(
            tokens.at[pl.ds(first_row, half_rows), pl.ds(column, own_rows)],
            x.at[:, pl.ds(p * own_rows, own_rows)],
            sems.at[3 + p],
        )
        copy.start()
        token_copies.append(copy)
    for copy in token_copies:
        copy.wait()
    part_copy = pltpu.make_async_copy(x, part, sems.at[3])
    part_copy.start()
    exp_copy.wait()
    base_copy.wait()
    trained_copy.wait()
    for i in range(row_blocks):
        for j in range(col_blocks):
            exponent = e[lax.rem(f * row_blocks, 8) + i, tp * col_blocks + j]
            scale = power(exponent)
            spot = (pl.ds(i * BLK, BLK), pl.ds(j * BLK, BLK))
            diff = t[spot].astype(jnp.float32) - b[spot].astype(jnp.float32)
            coded = jnp.clip(diff * (1.0 / scale), -clip_limit, clip_limit).astype(jnp.bfloat16)
            update[spot] = (coded.astype(jnp.float32) * (scale * lift)).astype(jnp.bfloat16)
    part_copy.wait()


def prepare(tokens, base, trained, exponents):
    rows, depth = tokens.shape
    half_rows, half = rows // 2, depth // 2
    own_rows, columns = trained.shape
    pairs = half // own_rows
    hbm = pl.BlockSpec(memory_space=pl.ANY)
    return pl.pallas_call(
        prepare_kernel,
        out_shape=(
            jax.ShapeDtypeStruct((own_rows, columns), jnp.bfloat16),
            jax.ShapeDtypeStruct((half_rows, half), jnp.bfloat16),
        ),
        in_specs=[hbm] * 4,
        out_specs=(pl.BlockSpec(memory_space=pltpu.VMEM), hbm),
        scratch_shapes=[
            pltpu.VMEM((half_rows, half), jnp.bfloat16),
            pltpu.VMEM((own_rows, columns), jnp.bfloat16),
            pltpu.VMEM((own_rows, columns), jnp.bfloat16),
            pltpu.SMEM((8, exponents.shape[1]), jnp.int32),
            pltpu.SemaphoreType.DMA((3 + pairs,)),
        ],
        compiler_params=pltpu.CompilerParams(vmem_limit_bytes=60 * 2**20),
        cost_estimate=pl.CostEstimate(flops=4 * 10**6, bytes_accessed=6 * 10**6, transcendentals=0),
    )(tokens, base, trained, exponents)


def far_kernel(base, delta, got, rest, gain, partial, total):
    step = pl.program_id(0)
    core = lax.rem(lax.axis_index("tp"), 2)
    half_rows = got.shape[0]

    @pl.when(step == 0)
    def _():
        total[...] = jnp.zeros_like(total)

    count, _, own_rows, columns = base.shape
    for i in range(count):
        spot = pl.ds(i * own_rows, own_rows)
        row = gain[pl.ds(pl.multiple_of((2 * (count * step + i) + lax.rem(lax.axis_index("fsdp"), 2)) * own_rows, own_rows), own_rows)].astype(jnp.float32).reshape(1, own_rows)
        weight = (base[i, 0].astype(jnp.float32) + delta[spot].astype(jnp.float32)).astype(jnp.bfloat16)
        for k, x in enumerate((got, rest)):
            raised = (x[:, spot].astype(jnp.float32) * row).astype(jnp.bfloat16)
            total[k] += jnp.dot(raised, weight, preferred_element_type=jnp.float32)

    @pl.when(step == pl.num_programs(0) - 1)
    def _():
        partial[pl.ds(pl.multiple_of(core * half_rows, 16), half_rows)] = total[0].astype(jnp.bfloat16)
        partial[pl.ds(pl.multiple_of((1 - core) * half_rows, 16), half_rows)] = total[1].astype(jnp.bfloat16)


def far_product(base4, delta, got, rest, gain4):
    pairs, _, own_rows, columns = base4.shape
    half_rows = got.shape[0]
    count = 2
    return pl.pallas_call(
        far_kernel,
        grid=(pairs // count,),
        out_shape=jax.ShapeDtypeStruct((2 * half_rows, columns), jnp.bfloat16),
        in_specs=[
            pl.BlockSpec((count, 1, own_rows, columns), lambda s: (s, lax.rem(lax.axis_index("fsdp"), 2), 0, 0)),
            pl.BlockSpec((count * own_rows, columns), lambda s: (s, 0)),
            pl.BlockSpec((half_rows, count * own_rows), lambda s: (0, s)),
            pl.BlockSpec((half_rows, count * own_rows), lambda s: (0, s)),
            pl.BlockSpec(gain4.shape, lambda s: (0,)),
        ],
        out_specs=pl.BlockSpec((2 * half_rows, columns), lambda s: (0, 0)),
        scratch_shapes=[pltpu.VMEM((2, half_rows, columns), jnp.float32)],
        compiler_params=pltpu.CompilerParams(vmem_limit_bytes=16 * 2**20),
        cost_estimate=pl.CostEstimate(flops=10**9, bytes_accessed=9 * 10**6, transcendentals=0),
    )(base4, delta, got, rest, gain4)


def factor_kernel(tokens, after, factor, squares):
    step = pl.program_id(0)

    @pl.when(step == 0)
    def _():
        squares[...] = jnp.zeros_like(squares)

    rows, width = tokens.shape
    found = squares[...]
    for c in range(width // BLK):
        wide = tokens[:, pl.ds(c * BLK, BLK)].astype(jnp.float32)
        found += wide * wide
    squares[...] = found

    @pl.when(step == pl.num_programs(0) - 1)
    def _():
        mean_square = jnp.sum(found, axis=1, keepdims=True) * (1.0 / (width * pl.num_programs(0)))
        factor[...] = jnp.broadcast_to(lax.rsqrt(mean_square + norm_epsilon), factor.shape)


def row_factor(tokens, after):
    rows, depth = tokens.shape
    steps = 4
    return pl.pallas_call(
        factor_kernel,
        grid=(steps,),
        out_shape=jax.ShapeDtypeStruct((rows, BLK), jnp.float32),
        in_specs=[pl.BlockSpec((rows, depth // steps), lambda s: (0, s)), pl.BlockSpec(memory_space=pl.ANY)],
        out_specs=pl.BlockSpec((rows, BLK), lambda s: (0, 0)),
        scratch_shapes=[pltpu.VMEM((rows, BLK), jnp.float32)],
        compiler_params=pltpu.CompilerParams(vmem_limit_bytes=16 * 2**20),
        cost_estimate=pl.CostEstimate(flops=5 * 10**6, bytes_accessed=5 * 10**6, transcendentals=0),
    )(tokens, after)


def near_kernel(base, delta, gain, factor, *refs):
    *tokens, product = refs
    step = pl.program_id(0)

    @pl.when(step == 0)
    def _():
        product[...] = jnp.zeros_like(product)

    count, _, own_rows, columns = base.shape
    scale = factor[:, :1]
    for i in range(count):
        spot = pl.ds(i * own_rows, own_rows)
        row = gain[pl.ds(pl.multiple_of((2 * (count * step + i) + lax.rem(lax.axis_index("fsdp"), 2)) * own_rows, own_rows), own_rows)].astype(jnp.float32).reshape(1, own_rows)
        weight = (base[i, 0].astype(jnp.float32) + delta[spot].astype(jnp.float32)).astype(jnp.bfloat16)
        normed = (tokens[i][...].astype(jnp.float32) * scale * row).astype(jnp.bfloat16)
        product[...] += jnp.dot(normed, weight, preferred_element_type=jnp.float32)


def near_product(tokens, gain4, base4, delta, factor):
    pairs, _, own_rows, columns = base4.shape
    rows, depth = tokens.shape
    count = 2

    def side():
        return lax.rem(lax.axis_index("fsdp"), 2)

    return pl.pallas_call(
        near_kernel,
        grid=(pairs // count,),
        out_shape=jax.ShapeDtypeStruct((rows, columns), jnp.float32),
        in_specs=[
            pl.BlockSpec((count, 1, own_rows, columns), lambda s: (s, side(), 0, 0)),
            pl.BlockSpec((count * own_rows, columns), lambda s: (s, 0)),
            pl.BlockSpec(gain4.shape, lambda s: (0,)),
            pl.BlockSpec((rows, BLK), lambda s: (0, 0)),
        ]
        + [pl.BlockSpec((rows, own_rows), lambda s, i=i: (0, 2 * (count * s + i) + side())) for i in range(count)],
        out_specs=pl.BlockSpec((rows, columns), lambda s: (0, 0)),
        compiler_params=pltpu.CompilerParams(vmem_limit_bytes=16 * 2**20),
        cost_estimate=pl.CostEstimate(flops=10**9, bytes_accessed=9 * 10**6, transcendentals=0),
    )(base4, delta, gain4, factor, *[tokens] * count)


def body(tokens, norm_gain, base, trained, exponents):
    rows, depth = tokens.shape
    columns = base.shape[1]
    own_rows = trained.shape[0]
    sides = depth // own_rows
    pairs = sides // 2
    across = [(i, i ^ 1) for i in range(sides)]
    cores = [(i, i ^ 1) for i in range(lax.axis_size("tp"))]
    groups = [list(range(0, sides, 2)), list(range(1, sides, 2))]
    update, part = prepare(tokens, base, trained, exponents)
    got = lax.ppermute(part, "fsdp", across)
    wide = lax.all_gather(update.astype(jnp.float16), "fsdp", axis=0, tiled=True, axis_index_groups=groups)
    wide, got = lax.optimization_barrier((wide, got))
    late_gain = norm_gain
    gain4 = late_gain
    rest = lax.ppermute(got, "tp", cores)
    delta = (wide.astype(jnp.float32) * (1.0 / lift)).astype(jnp.bfloat16)
    base4 = base.reshape(pairs, 2, own_rows, columns)
    partial = far_product(base4, delta, got, rest, gain4)
    far = lax.ppermute(partial, "fsdp", across)
    factor = row_factor(tokens, partial)
    near = near_product(tokens, gain4, base4, delta, factor)
    product = near + far.astype(jnp.float32) * factor[:, :1]
    return jax.nn.silu(product).astype(jnp.bfloat16)


def solution(mesh):
    placed = (P("fsdp", None), P(), P(None, "tp"), P("fsdp", "tp"), P())
    return jax.shard_map(
        body, mesh=mesh, in_specs=placed, out_specs=P("fsdp", "tp"), check_vma=False
    )
```

```python
from functools import partial as partial_of

import jax
import jax.numpy as jnp
from jax import lax
from jax.experimental import pallas as pl
from jax.experimental.pallas import tpu as pltpu
from jax.sharding import PartitionSpec as P

BLK = 128

clip_limit = 448.0
norm_epsilon = 1e-06
exponent_floor = -19
lift = 2.0**21

VMEM = pl.BlockSpec(memory_space=pltpu.VMEM)


def near_memory(x):
    return pltpu.with_memory_space_constraint(x, pltpu.VMEM)


def far_memory(x):
    return pltpu.with_memory_space_constraint(x, pltpu.HBM)


def power(exponent):
    scale = jnp.float32(2.0**exponent_floor)
    for level in range(exponent_floor + 1, exponent_floor + 6):
        scale = jnp.where(exponent == level, jnp.float32(2.0**level), scale)
    return scale


def prepare_kernel(tokens, base, trained, exponents, update, part, b, t, e, sems):
    own_rows, columns = trained.shape
    half_rows, half = part.shape
    pairs = half // own_rows
    f = lax.axis_index("fsdp")
    tp = lax.axis_index("tp")
    side = lax.rem(f, 2)
    core = lax.rem(tp, 2)
    row_blocks, col_blocks = own_rows // BLK, columns // BLK
    first_row = pl.multiple_of(core * half_rows, 16)
    exp_row = pl.multiple_of((f * row_blocks) // 8 * 8, 8)
    exp_copy = pltpu.make_async_copy(exponents.at[pl.ds(exp_row, 8)], e, sems.at[0])
    exp_copy.start()
    base_copy = pltpu.make_async_copy(base.at[pl.ds(pl.multiple_of(f * own_rows, own_rows), own_rows)], b, sems.at[1])
    base_copy.start()
    trained_copy = pltpu.make_async_copy(trained, t, sems.at[2])
    trained_copy.start()
    token_copies = []
    for p in range(pairs):
        column = pl.multiple_of((2 * p + 1 - side) * own_rows, own_rows)
        copy = pltpu.make_async_copy(
            tokens.at[pl.ds(first_row, half_rows), pl.ds(column, own_rows)],
            part.at[:, pl.ds(p * own_rows, own_rows)],
            sems.at[3 + p],
        )
        copy.start()
        token_copies.append(copy)
    exp_copy.wait()
    base_copy.wait()
    trained_copy.wait()
    for i in range(row_blocks):
        for j in range(col_blocks):
            exponent = e[lax.rem(f * row_blocks, 8) + i, tp * col_blocks + j]
            scale = power(exponent)
            spot = (pl.ds(i * BLK, BLK), pl.ds(j * BLK, BLK))
            diff = t[spot].astype(jnp.float32) - b[spot].astype(jnp.float32)
            coded = jnp.clip(diff * (1.0 / scale), -clip_limit, clip_limit).astype(jnp.bfloat16)
            update[spot] = (coded.astype(jnp.float32) * (scale * lift)).astype(jnp.bfloat16)
    for copy in token_copies:
        copy.wait()


def prepare(tokens, base, trained, exponents):
    rows, depth = tokens.shape
    half_rows, half = rows // 2, depth // 2
    own_rows, columns = trained.shape
    pairs = half // own_rows
    hbm = pl.BlockSpec(memory_space=pltpu.HBM)
    return pl.pallas_call(
        prepare_kernel,
        out_shape=(pltpu.VMEM((own_rows, columns), jnp.bfloat16), pltpu.VMEM((half_rows, half), jnp.bfloat16)),
        in_specs=[hbm] * 4,
        out_specs=(VMEM, VMEM),
        scratch_shapes=[
            pltpu.VMEM((own_rows, columns), jnp.bfloat16),
            pltpu.VMEM((own_rows, columns), jnp.bfloat16),
            pltpu.SMEM((8, exponents.shape[1]), jnp.int32),
            pltpu.SemaphoreType.DMA((3 + pairs,)),
        ],
        compiler_params=pltpu.CompilerParams(vmem_limit_bytes=16 * 2**20),
        cost_estimate=pl.CostEstimate(flops=4 * 10**6, bytes_accessed=3 * 10**6, transcendentals=0),
    )(*map(far_memory, (tokens, base, trained, exponents)))


def gain_row(gain, p, own_rows):
    side = lax.rem(lax.axis_index("fsdp"), 2)
    spot = pl.ds(pl.multiple_of((2 * p + side) * own_rows, own_rows), own_rows)
    return gain[spot].astype(jnp.float32).reshape(1, own_rows)


def first_kernel(base, delta, got, gain, weight, first):
    side = lax.rem(lax.axis_index("fsdp"), 2)
    pairs, _, own_rows, columns = base.shape
    total = jnp.zeros(first.shape, jnp.float32)
    for p in range(pairs):
        spot = pl.ds(p * own_rows, own_rows)
        block = (base[p, side].astype(jnp.float32) + delta[spot].astype(jnp.float32)).astype(jnp.bfloat16)
        weight[spot] = block
        raised = (got[:, spot].astype(jnp.float32) * gain_row(gain, p, own_rows)).astype(jnp.bfloat16)
        total += jnp.dot(raised, block, preferred_element_type=jnp.float32)
    first[...] = total.astype(jnp.bfloat16)


def second_kernel(own_rows, weight, rest, gain, first, partial):
    core = lax.rem(lax.axis_index("tp"), 2)
    half_rows, half = rest.shape
    total = jnp.zeros(first.shape, jnp.float32)
    for p in range(half // own_rows):
        spot = pl.ds(p * own_rows, own_rows)
        raised = (rest[:, spot].astype(jnp.float32) * gain_row(gain, p, own_rows)).astype(jnp.bfloat16)
        total += jnp.dot(raised, weight[spot], preferred_element_type=jnp.float32)
    partial[pl.ds(pl.multiple_of(core * half_rows, 16), half_rows)] = first[...]
    partial[pl.ds(pl.multiple_of((1 - core) * half_rows, 16), half_rows)] = total.astype(jnp.bfloat16)


def near_kernel(own_rows, tokens, weight, gain, after, product, factor):
    side = lax.rem(lax.axis_index("fsdp"), 2)
    rows, depth = tokens.shape
    squares = jnp.zeros((rows, BLK), jnp.float32)
    for c in range(depth // BLK):
        wide = tokens[:, pl.ds(c * BLK, BLK)].astype(jnp.float32)
        squares += wide * wide
    scale = lax.rsqrt(jnp.sum(squares, axis=1, keepdims=True) * (1.0 / depth) + norm_epsilon)
    factor[...] = jnp.broadcast_to(scale, factor.shape)
    total = jnp.zeros(product.shape, jnp.float32)
    for p in range(weight.shape[0] // own_rows):
        spot = pl.ds(pl.multiple_of((2 * p + side) * own_rows, own_rows), own_rows)
        normed = (tokens[:, spot].astype(jnp.float32) * scale * gain_row(gain, p, own_rows)).astype(jnp.bfloat16)
        total += jnp.dot(normed, weight[pl.ds(p * own_rows, own_rows)], preferred_element_type=jnp.float32)
    product[...] = total


def call(kernel, out_shape, flops, *operands, extra=()):
    many = isinstance(out_shape, tuple)
    return pl.pallas_call(
        kernel,
        out_shape=out_shape,
        in_specs=[VMEM] * len(operands) + [pl.BlockSpec(memory_space=pl.ANY)] * len(extra),
        out_specs=(VMEM,) * len(out_shape) if many else VMEM,
        compiler_params=pltpu.CompilerParams(vmem_limit_bytes=16 * 2**20),
        cost_estimate=pl.CostEstimate(flops=flops, bytes_accessed=8 * 10**6, transcendentals=0),
    )(*map(near_memory, operands), *extra)


def body(tokens, norm_gain, base, trained, exponents):
    rows, depth = tokens.shape
    columns = base.shape[1]
    own_rows = trained.shape[0]
    sides = depth // own_rows
    pairs = sides // 2
    half_rows, half = rows // 2, depth // 2
    across = [(i, i ^ 1) for i in range(sides)]
    cores = [(i, i ^ 1) for i in range(lax.axis_size("tp"))]
    groups = [list(range(0, sides, 2)), list(range(1, sides, 2))]
    update, part = prepare(tokens, base, trained, exponents)
    got = lax.ppermute(part, "fsdp", across)
    wide = lax.all_gather(update.astype(jnp.float16), "fsdp", axis=0, tiled=True, axis_index_groups=groups)
    wide, got = lax.optimization_barrier((wide, got))
    rest = lax.ppermute(got, "tp", cores)
    delta = (wide.astype(jnp.float32) * (1.0 / lift)).astype(jnp.bfloat16)
    base4 = base.reshape(pairs, 2, own_rows, columns)
    weight, first = call(
        first_kernel,
        (pltpu.VMEM((half, columns), jnp.bfloat16), pltpu.VMEM((half_rows, columns), jnp.bfloat16)),
        5 * 10**8,
        base4,
        delta,
        got,
        norm_gain,
    )
    partial = call(
        partial_of(second_kernel, own_rows), pltpu.VMEM((rows, columns), jnp.bfloat16), 5 * 10**8, weight, rest, norm_gain, first
    )
    far = lax.ppermute(partial, "fsdp", across)

    near, factor = call(
        partial_of(near_kernel, own_rows),
        (pltpu.VMEM((rows, columns), jnp.float32), pltpu.VMEM((rows, BLK), jnp.float32)),
        10**9,
        tokens,
        weight,
        norm_gain,
        extra=(partial,),
    )
    product = near + far.astype(jnp.float32) * factor[:, :1]
    return jax.nn.silu(product).astype(jnp.bfloat16)


def solution(mesh):
    placed = (P("fsdp", None), P(), P(None, "tp"), P("fsdp", "tp"), P())
    return jax.shard_map(
        body, mesh=mesh, in_specs=placed, out_specs=P("fsdp", "tp"), check_vma=False
    )
```

```python
from functools import partial as partial_of

import jax
import jax.numpy as jnp
from jax import lax
from jax.experimental import pallas as pl
from jax.experimental.pallas import tpu as pltpu
from jax.sharding import PartitionSpec as P

BLK = 128

clip_limit = 448.0
norm_epsilon = 1e-06
exponent_floor = -19
lift = 2.0**21

VMEM = pl.BlockSpec(memory_space=pltpu.VMEM)


def near_memory(x):
    return pltpu.with_memory_space_constraint(x, pltpu.VMEM)


def far_memory(x):
    return pltpu.with_memory_space_constraint(x, pltpu.HBM)


def power(exponent):
    scale = jnp.float32(2.0**exponent_floor)
    for level in range(exponent_floor + 1, exponent_floor + 6):
        scale = jnp.where(exponent == level, jnp.float32(2.0**level), scale)
    return scale


def prepare_kernel(tokens, base, trained, exponents, update, part, b, t, e, sems):
    own_rows, columns = trained.shape
    half_rows, half = part.shape
    pairs = half // own_rows
    f = lax.axis_index("fsdp")
    tp = lax.axis_index("tp")
    side = lax.rem(f, 2)
    core = lax.rem(tp, 2)
    row_blocks, col_blocks = own_rows // BLK, columns // BLK
    first_row = pl.multiple_of(core * half_rows, 16)
    exp_row = pl.multiple_of((f * row_blocks) // 8 * 8, 8)
    exp_copy = pltpu.make_async_copy(exponents.at[pl.ds(exp_row, 8)], e, sems.at[0])
    exp_copy.start()
    base_copy = pltpu.make_async_copy(base.at[pl.ds(pl.multiple_of(f * own_rows, own_rows), own_rows)], b, sems.at[1])
    base_copy.start()
    trained_copy = pltpu.make_async_copy(trained, t, sems.at[2])
    trained_copy.start()
    token_copies = []
    for p in range(pairs):
        column = pl.multiple_of((2 * p + 1 - side) * own_rows, own_rows)
        copy = pltpu.make_async_copy(
            tokens.at[pl.ds(first_row, half_rows), pl.ds(column, own_rows)],
            part.at[:, pl.ds(p * own_rows, own_rows)],
            sems.at[3 + p],
        )
        copy.start()
        token_copies.append(copy)
    exp_copy.wait()
    base_copy.wait()
    trained_copy.wait()
    for i in range(row_blocks):
        for j in range(col_blocks):
            exponent = e[lax.rem(f * row_blocks, 8) + i, tp * col_blocks + j]
            scale = power(exponent)
            spot = (pl.ds(i * BLK, BLK), pl.ds(j * BLK, BLK))
            diff = t[spot].astype(jnp.float32) - b[spot].astype(jnp.float32)
            coded = jnp.clip(diff * (1.0 / scale), -clip_limit, clip_limit).astype(jnp.bfloat16)
            update[spot] = (coded.astype(jnp.float32) * (scale * lift)).astype(jnp.bfloat16)
    for copy in token_copies:
        copy.wait()


def prepare(tokens, base, trained, exponents):
    rows, depth = tokens.shape
    half_rows, half = rows // 2, depth // 2
    own_rows, columns = trained.shape
    pairs = half // own_rows
    hbm = pl.BlockSpec(memory_space=pltpu.HBM)
    return pl.pallas_call(
        prepare_kernel,
        out_shape=(pltpu.VMEM((own_rows, columns), jnp.bfloat16), pltpu.VMEM((half_rows, half), jnp.bfloat16)),
        in_specs=[hbm] * 4,
        out_specs=(VMEM, VMEM),
        scratch_shapes=[
            pltpu.VMEM((own_rows, columns), jnp.bfloat16),
            pltpu.VMEM((own_rows, columns), jnp.bfloat16),
            pltpu.SMEM((8, exponents.shape[1]), jnp.int32),
            pltpu.SemaphoreType.DMA((3 + pairs,)),
        ],
        compiler_params=pltpu.CompilerParams(vmem_limit_bytes=16 * 2**20),
        cost_estimate=pl.CostEstimate(flops=4 * 10**6, bytes_accessed=3 * 10**6, transcendentals=0),
    )(*map(far_memory, (tokens, base, trained, exponents)))


def gain_row(gain, p, own_rows):
    side = lax.rem(lax.axis_index("fsdp"), 2)
    spot = pl.ds(pl.multiple_of((2 * p + side) * own_rows, own_rows), own_rows)
    return gain[spot].astype(jnp.float32).reshape(1, own_rows)


def first_kernel(base, delta, got, gain, weight, first):
    side = lax.rem(lax.axis_index("fsdp"), 2)
    pairs, _, own_rows, columns = base.shape
    total = jnp.zeros(first.shape, jnp.float32)
    for p in range(pairs):
        spot = pl.ds(p * own_rows, own_rows)
        block = (base[p, side].astype(jnp.float32) + delta[spot].astype(jnp.float32)).astype(jnp.bfloat16)
        weight[spot] = block
        raised = (got[:, spot].astype(jnp.float32) * gain_row(gain, p, own_rows)).astype(jnp.bfloat16)
        total += jnp.dot(raised, block, preferred_element_type=jnp.float32)
    first[...] = total.astype(jnp.bfloat16)


def second_kernel(own_rows, weight, rest, gain, first, partial):
    core = lax.rem(lax.axis_index("tp"), 2)
    half_rows, half = rest.shape
    raised = [
        (rest[:, pl.ds(p * own_rows, own_rows)].astype(jnp.float32) * gain_row(gain, p, own_rows)).astype(jnp.bfloat16)
        for p in range(half // own_rows)
    ]
    total = jnp.dot(jnp.concatenate(raised, axis=1), weight[...], preferred_element_type=jnp.float32)
    partial[pl.ds(pl.multiple_of(core * half_rows, 16), half_rows)] = first[...]
    partial[pl.ds(pl.multiple_of((1 - core) * half_rows, 16), half_rows)] = total.astype(jnp.bfloat16)


def near_kernel(own_rows, tokens, weight, gain, after, product, factor):
    side = lax.rem(lax.axis_index("fsdp"), 2)
    rows, depth = tokens.shape
    squares = jnp.zeros((rows, BLK), jnp.float32)
    for c in range(depth // BLK):
        wide = tokens[:, pl.ds(c * BLK, BLK)].astype(jnp.float32)
        squares += wide * wide
    scale = lax.rsqrt(jnp.sum(squares, axis=1, keepdims=True) * (1.0 / depth) + norm_epsilon)
    factor[...] = jnp.broadcast_to(scale, factor.shape)
    total = jnp.zeros(product.shape, jnp.float32)
    for p in range(weight.shape[0] // own_rows):
        spot = pl.ds(pl.multiple_of((2 * p + side) * own_rows, own_rows), own_rows)
        normed = (tokens[:, spot].astype(jnp.float32) * scale * gain_row(gain, p, own_rows)).astype(jnp.bfloat16)
        total += jnp.dot(normed, weight[pl.ds(p * own_rows, own_rows)], preferred_element_type=jnp.float32)
    product[...] = total


def call(kernel, out_shape, flops, *operands, extra=()):
    many = isinstance(out_shape, tuple)
    return pl.pallas_call(
        kernel,
        out_shape=out_shape,
        in_specs=[VMEM] * len(operands) + [pl.BlockSpec(memory_space=pl.ANY)] * len(extra),
        out_specs=(VMEM,) * len(out_shape) if many else VMEM,
        compiler_params=pltpu.CompilerParams(vmem_limit_bytes=16 * 2**20),
        cost_estimate=pl.CostEstimate(flops=flops, bytes_accessed=8 * 10**6, transcendentals=0),
    )(*map(near_memory, operands), *extra)


def last_kernel(near, factor, far, out, done, sems):
    rows = done.shape[0]
    count = sems.shape[0]
    copies = []
    for i in range(count):
        spot = pl.ds(i * (rows // count), rows // count)
        product = near[spot] + far[spot].astype(jnp.float32) * factor[spot, :1]
        done[spot] = (product / (1.0 + jnp.exp(-product))).astype(jnp.bfloat16)
        copy = pltpu.make_async_copy(done.at[spot], out.at[spot], sems.at[i])
        copy.start()
        copies.append(copy)
    for copy in copies:
        copy.wait()


def last_step(near, factor, far):
    return pl.pallas_call(
        last_kernel,
        out_shape=jax.ShapeDtypeStruct(near.shape, jnp.bfloat16),
        in_specs=[VMEM] * 3,
        out_specs=pl.BlockSpec(memory_space=pl.ANY),
        scratch_shapes=[pltpu.VMEM(near.shape, jnp.bfloat16), pltpu.SemaphoreType.DMA((3,))],
        compiler_params=pltpu.CompilerParams(vmem_limit_bytes=16 * 2**20),
        cost_estimate=pl.CostEstimate(flops=10**6, bytes_accessed=10**6, transcendentals=10**5),
    )(*map(near_memory, (near, factor, far)))


def body(tokens, norm_gain, base, trained, exponents):
    rows, depth = tokens.shape
    columns = base.shape[1]
    own_rows = trained.shape[0]
    sides = depth // own_rows
    pairs = sides // 2
    half_rows, half = rows // 2, depth // 2
    across = [(i, i ^ 1) for i in range(sides)]
    cores = [(i, i ^ 1) for i in range(lax.axis_size("tp"))]
    groups = [list(range(0, sides, 2)), list(range(1, sides, 2))]
    update, part = prepare(tokens, base, trained, exponents)
    got = lax.ppermute(part, "fsdp", across)
    wide = lax.all_gather(update.astype(jnp.float16), "fsdp", axis=0, tiled=True, axis_index_groups=groups)
    wide, got = lax.optimization_barrier((wide, got))
    rest = lax.ppermute(got, "tp", cores)
    delta = (wide.astype(jnp.float32) * (1.0 / lift)).astype(jnp.bfloat16)
    base4 = base.reshape(pairs, 2, own_rows, columns)
    weight, first = call(
        first_kernel,
        (pltpu.VMEM((half, columns), jnp.bfloat16), pltpu.VMEM((half_rows, columns), jnp.bfloat16)),
        5 * 10**8,
        base4,
        delta,
        got,
        norm_gain,
    )
    partial = call(
        partial_of(second_kernel, own_rows), pltpu.VMEM((rows, columns), jnp.bfloat16), 5 * 10**8, weight, rest, norm_gain, first
    )
    far = lax.ppermute(partial, "fsdp", across)

    near, factor = call(
        partial_of(near_kernel, own_rows),
        (pltpu.VMEM((rows, columns), jnp.float32), pltpu.VMEM((rows, BLK), jnp.float32)),
        10**9,
        tokens,
        weight,
        norm_gain,
        extra=(partial,),
    )
    return last_step(near, factor, far)


def solution(mesh):
    placed = (P("fsdp", None), P(), P(None, "tp"), P("fsdp", "tp"), P())
    return jax.shard_map(
        body, mesh=mesh, in_specs=placed, out_specs=P("fsdp", "tp"), check_vma=False
    )
```

```python
from functools import partial as partial_of

import jax
import jax.numpy as jnp
from jax import lax
from jax.experimental import pallas as pl
from jax.experimental.pallas import tpu as pltpu
from jax.sharding import PartitionSpec as P

BLK = 128

clip_limit = 448.0
norm_epsilon = 1e-06
exponent_floor = -19
lift = 2.0**21

VMEM = pl.BlockSpec(memory_space=pltpu.VMEM)


def near_memory(x):
    return pltpu.with_memory_space_constraint(x, pltpu.VMEM)


def far_memory(x):
    return pltpu.with_memory_space_constraint(x, pltpu.HBM)


def power(exponent):
    scale = jnp.float32(2.0**exponent_floor)
    for level in range(exponent_floor + 1, exponent_floor + 6):
        scale = jnp.where(exponent == level, jnp.float32(2.0**level), scale)
    return scale


def prepare_kernel(tokens, base, trained, exponents, update, part, b, t, e, sems):
    own_rows, columns = trained.shape
    direct_rows, half = part.shape
    share = direct_rows // 2
    pairs = half // own_rows
    f = lax.axis_index("fsdp")
    tp = lax.axis_index("tp")
    side = lax.rem(f, 2)
    core = lax.rem(tp, 2)
    row_blocks, col_blocks = own_rows // BLK, columns // BLK
    exp_row = pl.multiple_of((f * row_blocks) // 8 * 8, 8)
    exp_copy = pltpu.make_async_copy(exponents.at[pl.ds(exp_row, 8)], e, sems.at[0])
    exp_copy.start()
    base_copy = pltpu.make_async_copy(base.at[pl.ds(pl.multiple_of(f * own_rows, own_rows), own_rows)], b, sems.at[1])
    base_copy.start()
    trained_copy = pltpu.make_async_copy(trained, t, sems.at[2])
    trained_copy.start()
    token_copies = []
    for p in range(pairs):
        column = pl.multiple_of((2 * p + 1 - side) * own_rows, own_rows)
        here = pl.ds(p * own_rows, own_rows)
        sem = sems.at[3 + p]
        whole = pltpu.make_async_copy(tokens.at[pl.ds(0, direct_rows), pl.ds(column, own_rows)], part.at[:, here], sem)

        @pl.when(core == 0)
        def _(whole=whole):
            whole.start()

        @pl.when(core == 1)
        def _(column=column, here=here, sem=sem):
            for k, row in enumerate((direct_rows, share)):
                pltpu.make_async_copy(
                    tokens.at[pl.ds(row, share), pl.ds(column, own_rows)], part.at[pl.ds(k * share, share), here], sem
                ).start()

        token_copies.append(whole)
    exp_copy.wait()
    base_copy.wait()
    trained_copy.wait()
    for i in range(row_blocks):
        for j in range(col_blocks):
            exponent = e[lax.rem(f * row_blocks, 8) + i, tp * col_blocks + j]
            scale = power(exponent)
            spot = (pl.ds(i * BLK, BLK), pl.ds(j * BLK, BLK))
            diff = t[spot].astype(jnp.float32) - b[spot].astype(jnp.float32)
            coded = jnp.clip(diff * (1.0 / scale), -clip_limit, clip_limit).astype(jnp.bfloat16)
            update[spot] = (coded.astype(jnp.float32) * (scale * lift)).astype(jnp.bfloat16)
    for copy in token_copies:
        copy.wait()


def prepare(tokens, base, trained, exponents):
    rows, depth = tokens.shape
    direct_rows, half = rows // 3 * 2, depth // 2
    own_rows, columns = trained.shape
    pairs = half // own_rows
    hbm = pl.BlockSpec(memory_space=pltpu.HBM)
    return pl.pallas_call(
        prepare_kernel,
        out_shape=(pltpu.VMEM((own_rows, columns), jnp.bfloat16), pltpu.VMEM((direct_rows, half), jnp.bfloat16)),
        in_specs=[hbm] * 4,
        out_specs=(VMEM, VMEM),
        scratch_shapes=[
            pltpu.VMEM((own_rows, columns), jnp.bfloat16),
            pltpu.VMEM((own_rows, columns), jnp.bfloat16),
            pltpu.SMEM((8, exponents.shape[1]), jnp.int32),
            pltpu.SemaphoreType.DMA((3 + pairs,)),
        ],
        compiler_params=pltpu.CompilerParams(vmem_limit_bytes=16 * 2**20),
        cost_estimate=pl.CostEstimate(flops=4 * 10**6, bytes_accessed=3 * 10**6, transcendentals=0),
    )(*map(far_memory, (tokens, base, trained, exponents)))


def gain_row(gain, p, own_rows):
    side = lax.rem(lax.axis_index("fsdp"), 2)
    spot = pl.ds(pl.multiple_of((2 * p + side) * own_rows, own_rows), own_rows)
    return gain[spot].astype(jnp.float32).reshape(1, own_rows)


def first_kernel(base, delta, got, gain, weight, first):
    side = lax.rem(lax.axis_index("fsdp"), 2)
    pairs, _, own_rows, columns = base.shape
    total = jnp.zeros(first.shape, jnp.float32)
    for p in range(pairs):
        spot = pl.ds(p * own_rows, own_rows)
        block = (base[p, side].astype(jnp.float32) + delta[spot].astype(jnp.float32)).astype(jnp.bfloat16)
        weight[spot] = block
        raised = (got[:, spot].astype(jnp.float32) * gain_row(gain, p, own_rows)).astype(jnp.bfloat16)
        total += jnp.dot(raised, block, preferred_element_type=jnp.float32)
    first[...] = total.astype(jnp.bfloat16)


def second_kernel(own_rows, weight, rest, gain, first, partial):
    core = lax.rem(lax.axis_index("tp"), 2)
    share, half = rest.shape
    raised = [
        (rest[:, pl.ds(p * own_rows, own_rows)].astype(jnp.float32) * gain_row(gain, p, own_rows)).astype(jnp.bfloat16)
        for p in range(half // own_rows)
    ]
    total = jnp.dot(jnp.concatenate(raised, axis=1), weight[...], preferred_element_type=jnp.float32)
    partial[pl.ds(pl.multiple_of(core * 2 * share, 16), share)] = first[:share]
    partial[pl.ds(share, share)] = first[share:]
    partial[pl.ds(pl.multiple_of((1 - core) * 2 * share, 16), share)] = total.astype(jnp.bfloat16)


def near_kernel(own_rows, tokens, weight, gain, after, product, factor):
    side = lax.rem(lax.axis_index("fsdp"), 2)
    rows, depth = tokens.shape
    squares = jnp.zeros((rows, BLK), jnp.float32)
    for c in range(depth // BLK):
        wide = tokens[:, pl.ds(c * BLK, BLK)].astype(jnp.float32)
        squares += wide * wide
    scale = lax.rsqrt(jnp.sum(squares, axis=1, keepdims=True) * (1.0 / depth) + norm_epsilon)
    factor[...] = jnp.broadcast_to(scale, factor.shape)
    total = jnp.zeros(product.shape, jnp.float32)
    for p in range(weight.shape[0] // own_rows):
        spot = pl.ds(pl.multiple_of((2 * p + side) * own_rows, own_rows), own_rows)
        normed = (tokens[:, spot].astype(jnp.float32) * scale * gain_row(gain, p, own_rows)).astype(jnp.bfloat16)
        total += jnp.dot(normed, weight[pl.ds(p * own_rows, own_rows)], preferred_element_type=jnp.float32)
    product[...] = total


def call(kernel, out_shape, flops, *operands, extra=()):
    many = isinstance(out_shape, tuple)
    return pl.pallas_call(
        kernel,
        out_shape=out_shape,
        in_specs=[VMEM] * len(operands) + [pl.BlockSpec(memory_space=pl.ANY)] * len(extra),
        out_specs=(VMEM,) * len(out_shape) if many else VMEM,
        compiler_params=pltpu.CompilerParams(vmem_limit_bytes=16 * 2**20),
        cost_estimate=pl.CostEstimate(flops=flops, bytes_accessed=8 * 10**6, transcendentals=0),
    )(*map(near_memory, operands), *extra)


def last_kernel(near, factor, far, out, done, sems):
    rows = done.shape[0]
    count = sems.shape[0]
    copies = []
    for i in range(count):
        spot = pl.ds(i * (rows // count), rows // count)
        product = near[spot] + far[spot].astype(jnp.float32) * factor[spot, :1]
        done[spot] = (product / (1.0 + jnp.exp(-product))).astype(jnp.bfloat16)
        copy = pltpu.make_async_copy(done.at[spot], out.at[spot], sems.at[i])
        copy.start()
        copies.append(copy)
    for copy in copies:
        copy.wait()


def last_step(near, factor, far):
    return pl.pallas_call(
        last_kernel,
        out_shape=jax.ShapeDtypeStruct(near.shape, jnp.bfloat16),
        in_specs=[VMEM] * 3,
        out_specs=pl.BlockSpec(memory_space=pl.ANY),
        scratch_shapes=[pltpu.VMEM(near.shape, jnp.bfloat16), pltpu.SemaphoreType.DMA((3,))],
        compiler_params=pltpu.CompilerParams(vmem_limit_bytes=16 * 2**20),
        cost_estimate=pl.CostEstimate(flops=10**6, bytes_accessed=10**6, transcendentals=10**5),
    )(*map(near_memory, (near, factor, far)))


def body(tokens, norm_gain, base, trained, exponents):
    rows, depth = tokens.shape
    columns = base.shape[1]
    own_rows = trained.shape[0]
    sides = depth // own_rows
    pairs = sides // 2
    share, half = rows // 3, depth // 2
    across = [(i, i ^ 1) for i in range(sides)]
    cores = [(i, i ^ 1) for i in range(lax.axis_size("tp"))]
    groups = [list(range(0, sides, 2)), list(range(1, sides, 2))]
    update, part = prepare(tokens, base, trained, exponents)
    got = lax.ppermute(part, "fsdp", across)
    wide = lax.all_gather(update.astype(jnp.float16), "fsdp", axis=0, tiled=True, axis_index_groups=groups)
    wide, got = lax.optimization_barrier((wide, got))
    rest = lax.ppermute(got[:share], "tp", cores)
    delta = (wide.astype(jnp.float32) * (1.0 / lift)).astype(jnp.bfloat16)
    base4 = base.reshape(pairs, 2, own_rows, columns)
    weight, first = call(
        first_kernel,
        (pltpu.VMEM((half, columns), jnp.bfloat16), pltpu.VMEM((2 * share, columns), jnp.bfloat16)),
        5 * 10**8,
        base4,
        delta,
        got,
        norm_gain,
    )
    partial = call(
        partial_of(second_kernel, own_rows), pltpu.VMEM((rows, columns), jnp.bfloat16), 5 * 10**8, weight, rest, norm_gain, first
    )
    far = lax.ppermute(partial, "fsdp", across)

    near, factor = call(
        partial_of(near_kernel, own_rows),
        (pltpu.VMEM((rows, columns), jnp.float32), pltpu.VMEM((rows, BLK), jnp.float32)),
        10**9,
        tokens,
        weight,
        norm_gain,
        extra=(partial,),
    )
    return last_step(near, factor, far)


def solution(mesh):
    placed = (P("fsdp", None), P(), P(None, "tp"), P("fsdp", "tp"), P())
    return jax.shard_map(
        body, mesh=mesh, in_specs=placed, out_specs=P("fsdp", "tp"), check_vma=False
    )
```

```python
from functools import partial as partial_of

import jax
import jax.numpy as jnp
from jax import lax
from jax.experimental import pallas as pl
from jax.experimental.pallas import tpu as pltpu
from jax.sharding import PartitionSpec as P

BLK = 128

clip_limit = 448.0
norm_epsilon = 1e-06
exponent_floor = -19
lift = 2.0**21

VMEM = pl.BlockSpec(memory_space=pltpu.VMEM)


def near_memory(x):
    return pltpu.with_memory_space_constraint(x, pltpu.VMEM)


def far_memory(x):
    return pltpu.with_memory_space_constraint(x, pltpu.HBM)


def power(exponent):
    scale = jnp.float32(2.0**exponent_floor)
    for level in range(exponent_floor + 1, exponent_floor + 6):
        scale = jnp.where(exponent == level, jnp.float32(2.0**level), scale)
    return scale


def prepare_kernel(tokens, base, trained, exponents, update, part, b, t, e, sems):
    own_rows, columns = trained.shape
    half_rows, half = part.shape
    pairs = half // own_rows
    f = lax.axis_index("fsdp")
    tp = lax.axis_index("tp")
    side = lax.rem(f, 2)
    core = lax.rem(tp, 2)
    row_blocks, col_blocks = own_rows // BLK, columns // BLK
    first_row = pl.multiple_of(core * half_rows, 16)
    exp_row = pl.multiple_of((f * row_blocks) // 8 * 8, 8)
    exp_copy = pltpu.make_async_copy(exponents.at[pl.ds(exp_row, 8)], e, sems.at[0])
    exp_copy.start()
    base_copy = pltpu.make_async_copy(base.at[pl.ds(pl.multiple_of(f * own_rows, own_rows), own_rows)], b, sems.at[1])
    base_copy.start()
    trained_copy = pltpu.make_async_copy(trained, t, sems.at[2])
    trained_copy.start()
    token_copies = []
    for p in range(pairs):
        column = pl.multiple_of((2 * p + 1 - side) * own_rows, own_rows)
        copy = pltpu.make_async_copy(
            tokens.at[pl.ds(first_row, half_rows), pl.ds(column, own_rows)],
            part.at[:, pl.ds(p * own_rows, own_rows)],
            sems.at[3 + p],
        )
        copy.start(priority=p % 2)
        token_copies.append(copy)
    exp_copy.wait()
    base_copy.wait()
    trained_copy.wait()
    for i in range(row_blocks):
        for j in range(col_blocks):
            exponent = e[lax.rem(f * row_blocks, 8) + i, tp * col_blocks + j]
            scale = power(exponent)
            spot = (pl.ds(i * BLK, BLK), pl.ds(j * BLK, BLK))
            diff = t[spot].astype(jnp.float32) - b[spot].astype(jnp.float32)
            coded = jnp.clip(diff * (1.0 / scale), -clip_limit, clip_limit).astype(jnp.bfloat16)
            update[spot] = (coded.astype(jnp.float32) * (scale * lift)).astype(jnp.bfloat16)
    for copy in token_copies:
        copy.wait()


def prepare(tokens, base, trained, exponents):
    rows, depth = tokens.shape
    half_rows, half = rows // 2, depth // 2
    own_rows, columns = trained.shape
    pairs = half // own_rows
    hbm = pl.BlockSpec(memory_space=pltpu.HBM)
    return pl.pallas_call(
        prepare_kernel,
        out_shape=(pltpu.VMEM((own_rows, columns), jnp.bfloat16), pltpu.VMEM((half_rows, half), jnp.bfloat16)),
        in_specs=[hbm] * 4,
        out_specs=(VMEM, VMEM),
        scratch_shapes=[
            pltpu.VMEM((own_rows, columns), jnp.bfloat16),
            pltpu.VMEM((own_rows, columns), jnp.bfloat16),
            pltpu.SMEM((8, exponents.shape[1]), jnp.int32),
            pltpu.SemaphoreType.DMA((3 + pairs,)),
        ],
        compiler_params=pltpu.CompilerParams(vmem_limit_bytes=16 * 2**20),
        cost_estimate=pl.CostEstimate(flops=4 * 10**6, bytes_accessed=3 * 10**6, transcendentals=0),
    )(*map(far_memory, (tokens, base, trained, exponents)))


def gain_row(gain, p, own_rows):
    side = lax.rem(lax.axis_index("fsdp"), 2)
    spot = pl.ds(pl.multiple_of((2 * p + side) * own_rows, own_rows), own_rows)
    return gain[spot].astype(jnp.float32).reshape(1, own_rows)


def first_kernel(base, delta, got, gain, weight, first):
    side = lax.rem(lax.axis_index("fsdp"), 2)
    pairs, _, own_rows, columns = base.shape
    total = jnp.zeros(first.shape, jnp.float32)
    for p in range(pairs):
        spot = pl.ds(p * own_rows, own_rows)
        block = (base[p, side].astype(jnp.float32) + delta[spot].astype(jnp.float32)).astype(jnp.bfloat16)
        weight[spot] = block
        raised = (got[:, spot].astype(jnp.float32) * gain_row(gain, p, own_rows)).astype(jnp.bfloat16)
        total += jnp.dot(raised, block, preferred_element_type=jnp.float32)
    first[...] = total.astype(jnp.bfloat16)


def second_kernel(own_rows, weight, rest, gain, first, partial):
    core = lax.rem(lax.axis_index("tp"), 2)
    half_rows, half = rest.shape
    raised = [
        (rest[:, pl.ds(p * own_rows, own_rows)].astype(jnp.float32) * gain_row(gain, p, own_rows)).astype(jnp.bfloat16)
        for p in range(half // own_rows)
    ]
    total = jnp.dot(jnp.concatenate(raised, axis=1), weight[...], preferred_element_type=jnp.float32)
    partial[pl.ds(pl.multiple_of(core * half_rows, 16), half_rows)] = first[...]
    partial[pl.ds(pl.multiple_of((1 - core) * half_rows, 16), half_rows)] = total.astype(jnp.bfloat16)


def near_kernel(own_rows, tokens, weight, gain, after, product, factor):
    side = lax.rem(lax.axis_index("fsdp"), 2)
    rows, depth = tokens.shape
    squares = jnp.zeros((rows, BLK), jnp.float32)
    for c in range(depth // BLK):
        wide = tokens[:, pl.ds(c * BLK, BLK)].astype(jnp.float32)
        squares += wide * wide
    scale = lax.rsqrt(jnp.sum(squares, axis=1, keepdims=True) * (1.0 / depth) + norm_epsilon)
    factor[...] = jnp.broadcast_to(scale, factor.shape)
    total = jnp.zeros(product.shape, jnp.float32)
    for p in range(weight.shape[0] // own_rows):
        spot = pl.ds(pl.multiple_of((2 * p + side) * own_rows, own_rows), own_rows)
        normed = (tokens[:, spot].astype(jnp.float32) * scale * gain_row(gain, p, own_rows)).astype(jnp.bfloat16)
        total += jnp.dot(normed, weight[pl.ds(p * own_rows, own_rows)], preferred_element_type=jnp.float32)
    product[...] = total


def call(kernel, out_shape, flops, *operands, extra=()):
    many = isinstance(out_shape, tuple)
    return pl.pallas_call(
        kernel,
        out_shape=out_shape,
        in_specs=[VMEM] * len(operands) + [pl.BlockSpec(memory_space=pl.ANY)] * len(extra),
        out_specs=(VMEM,) * len(out_shape) if many else VMEM,
        compiler_params=pltpu.CompilerParams(vmem_limit_bytes=16 * 2**20),
        cost_estimate=pl.CostEstimate(flops=flops, bytes_accessed=8 * 10**6, transcendentals=0),
    )(*map(near_memory, operands), *extra)


def last_kernel(near, factor, far, out, done, sems):
    rows = done.shape[0]
    count = sems.shape[0]
    copies = []
    for i in range(count):
        spot = pl.ds(i * (rows // count), rows // count)
        product = near[spot] + far[spot].astype(jnp.float32) * factor[spot, :1]
        done[spot] = (product / (1.0 + jnp.exp(-product))).astype(jnp.bfloat16)
        copy = pltpu.make_async_copy(done.at[spot], out.at[spot], sems.at[i])
        copy.start()
        copies.append(copy)
    for copy in copies:
        copy.wait()


def last_step(near, factor, far):
    return pl.pallas_call(
        last_kernel,
        out_shape=jax.ShapeDtypeStruct(near.shape, jnp.bfloat16),
        in_specs=[VMEM] * 3,
        out_specs=pl.BlockSpec(memory_space=pl.ANY),
        scratch_shapes=[pltpu.VMEM(near.shape, jnp.bfloat16), pltpu.SemaphoreType.DMA((3,))],
        compiler_params=pltpu.CompilerParams(vmem_limit_bytes=16 * 2**20),
        cost_estimate=pl.CostEstimate(flops=10**6, bytes_accessed=10**6, transcendentals=10**5),
    )(*map(near_memory, (near, factor, far)))


def body(tokens, norm_gain, base, trained, exponents):
    rows, depth = tokens.shape
    columns = base.shape[1]
    own_rows = trained.shape[0]
    sides = depth // own_rows
    pairs = sides // 2
    half_rows, half = rows // 2, depth // 2
    across = [(i, i ^ 1) for i in range(sides)]
    cores = [(i, i ^ 1) for i in range(lax.axis_size("tp"))]
    groups = [list(range(0, sides, 2)), list(range(1, sides, 2))]
    update, part = prepare(tokens, base, trained, exponents)
    got = lax.ppermute(part, "fsdp", across)
    wide = lax.all_gather(update.astype(jnp.float16), "fsdp", axis=0, tiled=True, axis_index_groups=groups)
    wide, got = lax.optimization_barrier((wide, got))
    rest = lax.ppermute(got, "tp", cores)
    delta = (wide.astype(jnp.float32) * (1.0 / lift)).astype(jnp.bfloat16)
    base4 = base.reshape(pairs, 2, own_rows, columns)
    weight, first = call(
        first_kernel,
        (pltpu.VMEM((half, columns), jnp.bfloat16), pltpu.VMEM((half_rows, columns), jnp.bfloat16)),
        5 * 10**8,
        base4,
        delta,
        got,
        norm_gain,
    )
    partial = call(
        partial_of(second_kernel, own_rows), pltpu.VMEM((rows, columns), jnp.bfloat16), 5 * 10**8, weight, rest, norm_gain, first
    )
    far = lax.ppermute(partial, "fsdp", across)

    near, factor = call(
        partial_of(near_kernel, own_rows),
        (pltpu.VMEM((rows, columns), jnp.float32), pltpu.VMEM((rows, BLK), jnp.float32)),
        10**9,
        tokens,
        weight,
        norm_gain,
        extra=(partial,),
    )
    return last_step(near, factor, far)


def solution(mesh):
    placed = (P("fsdp", None), P(), P(None, "tp"), P("fsdp", "tp"), P())
    return jax.shard_map(
        body, mesh=mesh, in_specs=placed, out_specs=P("fsdp", "tp"), check_vma=False
    )
```
